32 devices in a mesh: gz: 4 (over z), rows: 8 (over y, x, core).
Axes of the slice: x: 2, y: 2, z: 4, core: 2. Of those that a mesh axis runs over, the one named last changes fastest.
Arguments:
- sections: bfloat16 [1, 4, 1024, 512], P(None, 'gz', 'rows'), may hold values from -6 to 6
- block_offset: int32 [1, 4, 8, 4], P(None, 'gz', 'rows'), may hold values from -3 to 3
- row_base: int32 [1, 4, 8, 4], P(None, 'gz', 'rows'), may hold values from 0 to 127
- col_base: int32 [1, 4, 8, 4], P(None, 'gz', 'rows'), may hold values from -128 to 127
- fractions: int32 [2, 1, 4, 8, 4], P(None, None, 'gz', 'rows'), may hold values from 0 to 255
- blend: float32 [1, 4], P(None, 'gz'), may hold values from 0.72 to 0.95
- conv_first: bfloat16 [9, 32, 2], replicated, may hold values from -1.5 to 1.5
- bias_first: float32 [32], replicated, may hold values from -3 to 3
- conv_down: bfloat16 [9, 32, 32], replicated, may hold values from -0.375 to 0.375
- bias_down: float32 [32], replicated, may hold values from -3 to 3
- conv_deep: bfloat16 [2, 9, 32, 32], replicated, may hold values from -0.375 to 0.375
- bias_deep: float32 [2, 32], replicated, may hold values from -3 to 3
Outputs:
- features: bfloat16 [1, 4, 32, 512, 256], P(None, 'gz', None, 'rows')
The draws below stay inside these ranges and needn't reach their ends.
All inputs are finite; a program needn't handle non-finite values.
Results may differ from the reference program's by a relative error of at most 0.001.
The reference program's roundings to bfloat16 on the way count: a program that leaves them out, or rounds other values in their place, can miss the bound.
Values may be sent and summed in bfloat16 or wider, within the bound.
A program may use at most 128 MiB of HBM per device.

```python
import math
import jax
import jax.numpy as jnp
from jax import lax

BLOCK = 128
REACH = 3
CHANNELS = 32
COL_BLOCKS = 4
CHAINS = 1
SECTIONS = 4
ROW_BLOCKS = 8
HEIGHT = 1024
WIDTH = 512


def touch_ends(entries, key, least, top_value):
    shape = entries.shape
    place = [jax.random.randint(jax.random.fold_in(key, axis), (), 0, shape[axis]) for axis in range(len(shape))]
    entries = entries.at[tuple(place)].set(least)
    longest = shape.index(max(shape))
    place[longest] = (place[longest] + 1) % shape[longest]
    return entries.at[tuple(place)].set(top_value)


def steps_of(stream_key, shape, cuts, least, high):
    def one(position, shards_of):
        draws = jax.random.uniform(jax.random.fold_in(jax.random.fold_in(stream_key, 6), position), (shards_of,), jnp.float32, least / len(cuts), high / len(cuts))
        return jnp.repeat(jnp.exp(draws), shape[position] // shards_of).reshape((-1,) + (1,) * (len(shape) - position - 1))

    loudness = one(*cuts[0])
    for cut in cuts[1:]:
        loudness = loudness * one(*cut)
    return loudness


def noise(rng, dims, scale, bound, cuts=(), kind=jnp.bfloat16):
    factor_of = steps_of(rng, dims, cuts, -0.22, 0.18) if cuts else 1.0
    values = jax.random.normal(rng, dims, jnp.float32) * scale * factor_of
    return jnp.minimum(jnp.maximum(values, -bound), bound).astype(kind)


def setup_inputs(seed: int = 0) -> dict:
    streams_of = jax.random.split(jax.random.key(seed), 13)
    return {
        "sections": noise(streams_of[0], (CHAINS, SECTIONS, HEIGHT, WIDTH), 1.0, 6.0, ((1, 4), (2, 8))),
        "block_offset": touch_ends(jax.random.randint(streams_of[1], (CHAINS, SECTIONS, ROW_BLOCKS, COL_BLOCKS), -REACH, REACH + 1), jax.random.fold_in(streams_of[1], 1), -REACH, REACH).astype(jnp.int32),
        "row_base": touch_ends(jax.random.randint(streams_of[2], (CHAINS, SECTIONS, ROW_BLOCKS, COL_BLOCKS), 0, BLOCK), jax.random.fold_in(streams_of[2], 1), 0, BLOCK - 1).astype(jnp.int32),
        "col_base": touch_ends(jax.random.randint(streams_of[3], (CHAINS, SECTIONS, ROW_BLOCKS, COL_BLOCKS), -BLOCK, BLOCK), jax.random.fold_in(streams_of[3], 1), -BLOCK, BLOCK - 1).astype(jnp.int32),
        "fractions": touch_ends(jax.random.randint(streams_of[4], (2, CHAINS, SECTIONS, ROW_BLOCKS, COL_BLOCKS), 0, 256), jax.random.fold_in(streams_of[4], 1), 0, 255).astype(jnp.int32),
        "blend": jnp.clip(jnp.exp(math.log(0.95) - 0.2772107 * jax.random.uniform(streams_of[5], (CHAINS, SECTIONS), jnp.float32) ** steps_of(streams_of[5], (CHAINS, SECTIONS), ((1, 4),), -0.2, 0.2)), 0.72, 0.95),
        "conv_first": noise(streams_of[6], (9, CHANNELS, 2), 18 ** -0.5, 1.5),
        "bias_first": noise(streams_of[7], (CHANNELS,), 0.5, 3.0, (), jnp.float32),
        "conv_down": noise(streams_of[8], (9, CHANNELS, CHANNELS), (9 * CHANNELS) ** -0.5, 0.375),
        "bias_down": noise(streams_of[9], (CHANNELS,), 0.5, 3.0, (), jnp.float32),
        "conv_deep": noise(streams_of[10], (2, 9, CHANNELS, CHANNELS), (9 * CHANNELS) ** -0.5, 0.375),
        "bias_deep": noise(streams_of[11], (2, CHANNELS), 0.5, 3.0, (), jnp.float32),
    }


def interp_rows(row_start, fraction):
    weight_hi = fraction.astype(jnp.float32) / 256.0
    out_idx = jnp.arange(BLOCK, dtype=jnp.int32)[:, None]
    src_idx = jnp.arange(2 * BLOCK, dtype=jnp.int32)[None, :]
    matrix = jnp.where(src_idx == out_idx + row_start, 1.0 - weight_hi, 0.0)
    matrix = matrix + jnp.where(src_idx == out_idx + row_start + 1, weight_hi, 0.0)
    return matrix.astype(jnp.bfloat16)


def interp_cols(fraction):
    weight_hi = fraction.astype(jnp.float32) / 256.0
    src_idx = jnp.arange(2 * BLOCK, dtype=jnp.int32)[:, None]
    out_idx = jnp.arange(BLOCK, dtype=jnp.int32)[None, :]
    matrix = jnp.where(src_idx == out_idx, 1.0 - weight_hi, 0.0)
    matrix = matrix + jnp.where(src_idx == out_idx + 1, weight_hi, 0.0)
    return matrix.astype(jnp.bfloat16)


def warp_one(padded, row_idx, col_idx, offset, row_start, col_start, frac_row, frac_col):
    first_row = ((row_idx + offset + REACH) * BLOCK).astype(jnp.int32)
    first_col = (col_idx * BLOCK + col_start + BLOCK).astype(jnp.int32)
    window = lax.dynamic_slice(padded, (first_row, first_col), (2 * BLOCK, 2 * BLOCK))
    moved_cols = jnp.dot(window, interp_cols(frac_col), preferred_element_type=jnp.float32).astype(jnp.bfloat16)
    return jnp.dot(interp_rows(row_start, frac_row), moved_cols, preferred_element_type=jnp.float32)


def warp_section(section, offset, row_start, col_start, fraction):
    padded = jnp.pad(section, ((REACH * BLOCK, (REACH + 1) * BLOCK), (BLOCK, 2 * BLOCK)))
    row_ids = jnp.broadcast_to(jnp.arange(ROW_BLOCKS, dtype=jnp.int32)[:, None], (ROW_BLOCKS, COL_BLOCKS)).reshape(-1)
    col_ids = jnp.broadcast_to(jnp.arange(COL_BLOCKS, dtype=jnp.int32)[None, :], (ROW_BLOCKS, COL_BLOCKS)).reshape(-1)
    blocks = jax.vmap(warp_one, in_axes=(None, 0, 0, 0, 0, 0, 0, 0))(
        padded, row_ids, col_ids, offset.reshape(-1), row_start.reshape(-1), col_start.reshape(-1),
        fraction[0].reshape(-1), fraction[1].reshape(-1))
    return blocks.reshape(ROW_BLOCKS, COL_BLOCKS, BLOCK, BLOCK).transpose(0, 2, 1, 3).reshape(HEIGHT, WIDTH)


def convolve(operand, kernel, stride, padding):
    weights = kernel.astype(jnp.float32).reshape(3, 3, kernel.shape[1], kernel.shape[2]).transpose(2, 3, 0, 1)
    result = lax.conv_general_dilated(operand.astype(jnp.float32)[None], weights, (stride, stride), padding,
                                      precision=lax.Precision.HIGHEST)
    return result[0]


def encode(warped_one, prior_one, conv_first, bias_first, conv_down, bias_down, conv_deep, bias_deep):
    same_pad = ((1, 1), (1, 1))
    encoder_in = jnp.stack([warped_one, prior_one]).astype(jnp.bfloat16)
    hidden = jax.nn.relu(convolve(encoder_in, conv_first, 1, same_pad) + bias_first[:, None, None]).astype(jnp.bfloat16)
    down = jax.nn.relu(convolve(hidden, conv_down, 2, ((1, 0), (1, 0))) + bias_down[:, None, None]).astype(jnp.bfloat16)
    deep = jax.nn.relu(convolve(down, conv_deep[0], 1, same_pad) + bias_deep[0][:, None, None]).astype(jnp.bfloat16)
    return (convolve(deep, conv_deep[1], 1, same_pad) + bias_deep[1][:, None, None]).astype(jnp.bfloat16)


def reference(sections, block_offset, row_base, col_base, fractions, blend, conv_first, bias_first, conv_down, bias_down, conv_deep, bias_deep):
    def one_chain(inputs):
        section_set, offsets, row_starts, col_starts, frac_set, decay = inputs
        warped = lax.map(lambda element: warp_section(*element), (section_set, offsets, row_starts, col_starts, frac_set))

        def blend_step(prior_ref, element):
            decay_rate, section = element
            return decay_rate * prior_ref + (1.0 - decay_rate) * section, prior_ref

        _, priors = lax.scan(blend_step, jnp.zeros((HEIGHT, WIDTH), jnp.float32), (decay, warped))
        return lax.map(lambda element: encode(element[0], element[1], conv_first, bias_first, conv_down, bias_down, conv_deep, bias_deep), (warped, priors))

    return lax.map(one_chain, (sections, block_offset, row_base, col_base, fractions.transpose(1, 2, 0, 3, 4), blend))
```

```python
import functools

import jax
import jax.numpy as jnp
import numpy as np
from jax import lax
from jax.experimental import pallas as pl
from jax.experimental.pallas import tpu as pltpu
from jax.sharding import PartitionSpec as P

REACH = 3
HALO = 8
FIRST_ROWS = 14
DOWN_ROWS = 4
DEEP_ROWS = 6
LAST_ROWS = 8
SLOTS = 16
LANES = 128
MESH = pl.DeviceIdType.MESH


def ceil_div(a, b):
    return -(-a // b)


def exchange_kernel(
    n_rows,
    n_gz,
    offset_ref,
    row_ref,
    col_ref,
    fraction_ref,
    blend_ref,
    section_ref,
    base_first_ref,
    base_ref,
    warped_ref,
    prior_ref,
    first_ref,
    down_ref,
    deep_ref,
    last_ref,
    source,
    warped,
    prior,
    state,
    sec_send,
    sec_recv,
    halo_send,
    halo_recv,
    chain_send,
    chain_recv,
):
    me = lax.axis_index("rows")
    z = lax.axis_index("gz")
    tile, width = section_ref.shape
    half = width // 2
    odd = lax.rem(me, 2)
    even = 1 - odd
    sibling = me + even - odd

    barrier = pltpu.get_barrier_semaphore()
    greeted = jnp.int32(0)
    for d in (-4, -3, -2, -1, 1, 2, 3, 4):
        ok = jnp.logical_and(me + d >= 0, me + d < n_rows)

        @pl.when(ok)
        def _(d=d):
            pl.semaphore_signal(barrier, inc=1, device_id=(z, me + d), device_id_type=MESH)

        greeted = greeted + jnp.where(ok, 1, 0)
    for d in (-1, 1):
        ok = jnp.logical_and(z + d >= 0, z + d < n_gz)

        @pl.when(ok)
        def _(d=d):
            pl.semaphore_signal(barrier, inc=1, device_id=(z + d, me), device_id_type=MESH)

        greeted = greeted + jnp.where(ok, 1, 0)

    source[REACH] = section_ref[...]
    pl.semaphore_wait(barrier, greeted)

    def send(src_slot, dst_slot, target):
        return pltpu.make_async_remote_copy(
            src_ref=source.at[src_slot],
            dst_ref=source.at[dst_slot],
            send_sem=sec_send.at[dst_slot],
            recv_sem=sec_recv.at[dst_slot],
            device_id=(z, target),
            device_id_type=MESH,
        )

    def inside(k):
        return jnp.logical_and(k >= 0, k < n_rows)

    direct = []
    for slot in (5, 1, 7):
        target = me - (slot - REACH)
        direct.append((inside(target), send(REACH, slot, target)))
    direct.append((jnp.logical_and(odd == 1, inside(me + 3)), send(REACH, 0, me + 3)))
    relay_even = {s: (jnp.logical_and(even == 1, inside(me + s - REACH)), send(s, s - 1, sibling)) for s in (3, 5, 1, 7)}
    relay_odd = {s: (jnp.logical_and(odd == 1, inside(me + s - REACH)), send(s, s + 1, sibling)) for s in (3, 5, 1)}
    sends = direct + list(relay_even.values()) + list(relay_odd.values())

    for ok, copy in direct + [relay_even[3], relay_odd[3]]:

        @pl.when(ok)
        def _(copy=copy):
            copy.start()

    for slot in range(2 * REACH + 2):
        if slot != REACH:

            @pl.when(jnp.logical_not(inside(me + slot - REACH)))
            def _(slot=slot):
                source[slot] = jnp.zeros((tile, width), source.dtype)

    def arrive(slot):
        @pl.when(inside(me + slot - REACH))
        def _():
            send(slot, slot, sibling).wait_recv()

    def weights():
        base = base_first_ref[...]
        rows = base.shape[0]
        for r in range(FIRST_ROWS):
            moved = base if r == 0 else pltpu.roll(base, SLOTS * r, 1)
            first_ref[r * rows : (r + 1) * rows, :] = moved.astype(jnp.bfloat16)
        channels = base_ref.shape[1]
        triple = 3 * channels
        for ref, layer, count, step in ((down_ref, 0, DOWN_ROWS, 2), (deep_ref, 1, DEEP_ROWS, 1)):
            base = base_ref[layer]
            for r in range(count):
                moved = base if r == 0 else pltpu.roll(base, triple * step * r, 1)
                ref[r * channels : (r + 1) * channels, :] = moved[:, : ref.shape[1]].astype(jnp.bfloat16)
        base = base_ref[2]
        pieces = [base if r == 0 else pltpu.roll(base, triple * r, 1) for r in range(LAST_ROWS)]
        last = jnp.stack(pieces, axis=1).reshape(channels * LAST_ROWS, base.shape[1])
        last_ref[...] = last[:, : last_ref.shape[1]].astype(jnp.bfloat16)

    weights()

    for slot in (5, 1, 7):
        arrive(slot)

        @pl.when(relay_even[slot][0])
        def _(slot=slot):
            relay_even[slot][1].start()

        if slot in relay_odd:

            @pl.when(relay_odd[slot][0])
            def _(slot=slot):
                relay_odd[slot][1].start()

    for slot in (4, 2, 0, 6):
        arrive(slot)

    col_tiles = width // tile
    for m in range(col_tiles // 2):
        row_parts = []
        moved_parts = []
        for side in range(2):
            j = 2 * m + side
            a = row_ref[0, 0, 0, j]
            b = col_ref[0, 0, 0, j]
            p = fraction_ref[0, 0, 0, 0, j].astype(jnp.float32) / 256.0
            q = fraction_ref[1, 0, 0, 0, j].astype(jnp.float32) / 256.0
            low = max(j - 1, 0) * tile
            high = min(j + 2, col_tiles) * tile
            window = source[pl.ds(offset_ref[0, 0, 0, j] + REACH, 2), :, low:high].reshape(2 * tile, high - low)
            src = lax.broadcasted_iota(jnp.int32, (high - low, 2 * tile), 0) + low
            lane = lax.broadcasted_iota(jnp.int32, (high - low, 2 * tile), 1)
            is_odd = lane >= tile
            place = jnp.where(is_odd, lane - tile, lane) - side * (tile // 2)
            here = jnp.logical_and(place >= 0, place < tile // 2)
            want = jnp.where(here, 2 * place + jnp.where(is_odd, 1, 0) + (j * tile + b), -(1 << 20))
            delta = src - want
            col_matrix = jnp.where(delta == 0, 1.0 - q, 0.0) + jnp.where(delta == 1, q, 0.0)
            moved = jnp.dot(window, col_matrix.astype(jnp.bfloat16), preferred_element_type=jnp.float32)
            moved_parts.append(moved.astype(jnp.bfloat16))
            delta = (
                lax.broadcasted_iota(jnp.int32, (tile, 2 * tile), 1)
                - lax.broadcasted_iota(jnp.int32, (tile, 2 * tile), 0)
                - a
            )
            row_matrix = jnp.where(delta == 0, 1.0 - p, 0.0) + jnp.where(delta == 1, p, 0.0)
            row_parts.append(row_matrix.astype(jnp.bfloat16))
        block = jnp.dot(
            jnp.concatenate(row_parts, axis=1),
            jnp.concatenate(moved_parts, axis=0),
            preferred_element_type=jnp.float32,
        )
        warped[HALO : HALO + tile, m * tile : (m + 1) * tile] = block[:, :tile]
        warped[HALO : HALO + tile, half + m * tile : half + (m + 1) * tile] = block[:, tile:]

    top = pl.ds(0, HALO)
    bottom = pl.ds(HALO + tile, HALO)

    def edge(index, src, dst, target):
        return pltpu.make_async_remote_copy(
            src_ref=warped.at[src],
            dst_ref=warped.at[dst],
            send_sem=halo_send.at[index],
            recv_sem=halo_recv.at[index],
            device_id=(z, target),
            device_id_type=MESH,
        )

    up = edge(0, pl.ds(HALO, HALO), bottom, me - 1)
    down = edge(1, pl.ds(tile, HALO), top, me + 1)
    has_up = me > 0
    has_down = me < n_rows - 1

    @pl.when(has_up)
    def _():
        up.start()

    @pl.when(has_down)
    def _():
        down.start()

    @pl.when(jnp.logical_not(has_up))
    def _():
        warped[top, :] = jnp.zeros((HALO, width), jnp.float32)

    @pl.when(jnp.logical_not(has_down))
    def _():
        warped[bottom, :] = jnp.zeros((HALO, width), jnp.float32)

    keep = blend_ref[0, 0]
    pieces = chain_send.shape[0] - 2
    length = tile // pieces
    chunks = [pl.ds(HALO + c * length, length) for c in range(pieces)] + [top, bottom]
    has_before = z > 0
    has_after = z < n_gz - 1

    def pass_on(index, chunk):
        return pltpu.make_async_remote_copy(
            src_ref=state.at[chunk],
            dst_ref=prior.at[chunk],
            send_sem=chain_send.at[index],
            recv_sem=chain_recv.at[index],
            device_id=(z + 1, me),
            device_id_type=MESH,
        )

    for index, chunk in enumerate(chunks):
        if index == pieces:

            @pl.when(has_down)
            def _():
                up.wait_recv()

            @pl.when(has_up)
            def _():
                down.wait_recv()

        @pl.when(has_before)
        def _(index=index, chunk=chunk):
            pass_on(index, chunk).wait_recv()

        @pl.when(jnp.logical_not(has_before))
        def _(chunk=chunk):
            prior[chunk, :] = jnp.zeros((chunk.size, width), jnp.float32)

        @pl.when(has_after)
        def _(index=index, chunk=chunk):
            state[chunk, :] = keep * prior[chunk, :] + (1.0 - keep) * warped[chunk, :]
            pass_on(index, chunk).start()

    warped_ref[...] = warped[...]
    prior_ref[...] = prior[...]

    for ok, copy in sends:

        @pl.when(ok)
        def _(copy=copy):
            copy.wait_send()

    @pl.when(has_up)
    def _():
        up.wait_send()

    @pl.when(has_down)
    def _():
        down.wait_send()

    @pl.when(has_after)
    def _():
        for index, chunk in enumerate(chunks):
            pass_on(index, chunk).wait_send()


def encoder_kernel(
    n_rows,
    warped_ref,
    prior_ref,
    first_ref,
    down_ref,
    deep_ref,
    last_ref,
    bias_ref,
    out_ref,
    planes,
    hidden,
    down,
    deep,
):
    me = lax.axis_index("rows")
    is_top = me == 0
    is_bottom = me == n_rows - 1
    ext, width = warped_ref.shape
    tile = ext - 2 * HALO
    half = width // 2
    channels, out_rows, _ = out_ref.shape

    def put(slot, value):
        for h in range(half // LANES):
            planes[h, pl.ds(slot, ext, stride=SLOTS), :] = value[:, h * LANES : (h + 1) * LANES]

    lane = lax.broadcasted_iota(jnp.int32, (ext, half), 1)
    zero = jnp.zeros((ext, half), jnp.float32)
    one = jnp.ones((ext, half), jnp.float32)
    for ch, ref in enumerate((warped_ref, prior_ref)):
        e = ref[:, :half]
        o = ref[:, half:]
        put(ch, jnp.where(lane == 0, 0.0, pltpu.roll(e, 1, 1)))
        put(2 + ch, jnp.where(lane == 0, 0.0, pltpu.roll(o, 1, 1)))
        put(4 + ch, jnp.where(lane == 0, 0.0, e))
        put(6 + ch, e)
        put(8 + ch, o)
        put(10 + ch, jnp.where(lane == half - 1, 0.0, pltpu.roll(e, half - 1, 1)))
        put(12 + ch, one if ch == 0 else jnp.where(lane == 0, 0.0, one))
        put(14 + ch, zero)

    def first_group(g, _):
        start = pl.multiple_of((2 + FIRST_ROWS * g) * SLOTS, SLOTS)
        parts = [planes[h, pl.ds(start, SLOTS * (FIRST_ROWS + 2)), :] for h in range(half // LANES)]
        window = jnp.concatenate(parts, axis=1).astype(jnp.bfloat16)
        value = jnp.dot(first_ref[...], window, preferred_element_type=jnp.float32)
        value = jnp.maximum(value, 0.0).astype(jnp.bfloat16)
        hidden[pl.ds(g * FIRST_ROWS, FIRST_ROWS)] = value.reshape(FIRST_ROWS, 3 * channels, half)
        return 0

    lax.fori_loop(0, hidden.shape[0] // FIRST_ROWS, first_group, 0)

    def clear(ref, above, inner):
        @pl.when(is_top)
        def _():
            ref[0:above] = jnp.zeros((above,) + ref.shape[1:], ref.dtype)

        @pl.when(is_bottom)
        def _():
            below = ref.shape[0] - above - inner
            ref[above + inner :] = jnp.zeros((below,) + ref.shape[1:], ref.dtype)

    clear(hidden, 5, tile)

    def spread(ref, start, count, value):
        value = jnp.maximum(value, 0.0)
        lane = lax.broadcasted_iota(jnp.int32, value.shape, 1)
        left = jnp.where(lane == 0, 0.0, pltpu.roll(value, 1, 1))
        right = jnp.where(lane == half - 1, 0.0, pltpu.roll(value, half - 1, 1))
        for index, piece in enumerate((left, value, right)):
            ref[pl.ds(start, count), index * channels : (index + 1) * channels, :] = piece.astype(
                jnp.bfloat16
            ).reshape(count, channels, half)

    def biased(value, layer, count):
        return (value.reshape(count, channels, half) + bias_ref[layer][None]).reshape(count * channels, half)

    def down_group(g, _):
        window = hidden[pl.ds(2 * DOWN_ROWS * g, 2 * DOWN_ROWS + 1)].reshape(-1, half)
        value = jnp.dot(down_ref[...], window, preferred_element_type=jnp.float32)
        spread(down, g * DOWN_ROWS, DOWN_ROWS, biased(value, 0, DOWN_ROWS))
        return 0

    lax.fori_loop(0, down.shape[0] // DOWN_ROWS, down_group, 0)
    clear(down, 2, out_rows)

    def deep_group(g, _):
        window = down[pl.ds(DEEP_ROWS * g, DEEP_ROWS + 2)].reshape(-1, half)
        value = jnp.dot(deep_ref[...], window, preferred_element_type=jnp.float32)
        spread(deep, g * DEEP_ROWS, DEEP_ROWS, biased(value, 1, DEEP_ROWS))
        return 0

    lax.fori_loop(0, deep.shape[0] // DEEP_ROWS, deep_group, 0)
    clear(deep, 1, out_rows)

    for g in range(out_rows // (2 * LAST_ROWS)):
        parts = []
        for k in range(2):
            start = (2 * g + k) * LAST_ROWS
            window = deep[start : start + LAST_ROWS + 2].reshape(-1, half)
            value = jnp.dot(last_ref[...], window, preferred_element_type=jnp.float32)
            parts.append(value.reshape(channels, LAST_ROWS, half) + bias_ref[2][:, None, :])
        out_ref[:, 2 * g * LAST_ROWS : 2 * (g + 1) * LAST_ROWS, :] = jnp.concatenate(parts, axis=1).astype(
            jnp.bfloat16
        )


def first_base(conv_first, bias_first):
    channels = conv_first.shape[1]
    pick = np.zeros((3, 3, 8), np.float32)
    for plane, slots in enumerate(((0, 1, 2), (1, 3, 4), (3, 4, 5))):
        for tap, slot in enumerate(slots):
            pick[plane, tap, slot] = 1.0
    kernel = conv_first.astype(jnp.float32).reshape(3, 3, channels, 2)
    base = jnp.zeros((3, channels, 3, 8, 2), jnp.float32)
    for tap in range(3):
        base = base + pick[:, tap][:, None, None, :, None] * kernel[:, tap].transpose(1, 0, 2)[None, :, :, None, :]
    high = lax.reduce_precision(bias_first, 8, 7)
    middle = lax.reduce_precision(bias_first - high, 8, 7)
    low = bias_first - high - middle
    terms = jnp.stack([high, middle, low], axis=1)
    ones = np.zeros((3, 8, 2), np.float32)
    ones[1:, 6, 0] = 1.0
    ones[0, 6, 1] = 1.0
    base = base + terms[None, :, :, None, None] * ones[:, None, None]
    base = base.reshape(3 * channels, 3 * SLOTS)
    return jnp.pad(base, ((0, 0), (0, (FIRST_ROWS + 2) * SLOTS - 3 * SLOTS)))


def per_device(
    n_rows,
    n_gz,
    sections,
    block_offset,
    row_base,
    col_base,
    fractions,
    blend,
    conv_first,
    bias_first,
    conv_down,
    bias_down,
    conv_deep,
    bias_deep,
):
    section = sections[0, 0]
    tile, width = section.shape
    half = width // 2
    out_rows = tile // 2
    channels = conv_first.shape[1]
    triple = 3 * channels
    ext = tile + 2 * HALO
    kernels = jnp.concatenate([conv_down[None], conv_deep], axis=0)
    lanes = ceil_div(triple * (LAST_ROWS + 2), 128) * 128
    base = kernels.transpose(0, 2, 1, 3).reshape(3, channels, 9 * channels).astype(jnp.float32)
    base = jnp.pad(base, ((0, 0), (0, 0), (0, lanes - 9 * channels)))
    biases = jnp.concatenate([bias_down[None], bias_deep], axis=0)
    biases = jnp.broadcast_to(biases[:, :, None], (3, channels, half))
    base_first = first_base(conv_first, bias_first)
    first_lanes = base_first.shape[1]

    vmem = pl.BlockSpec(memory_space=pltpu.VMEM)
    smem = pl.BlockSpec(memory_space=pltpu.SMEM)
    pieces = 4
    f32 = jnp.float32
    bf16 = jnp.bfloat16
    shape = jax.ShapeDtypeStruct
    warped, prior, first, down, deep, last = pl.pallas_call(
        functools.partial(exchange_kernel, n_rows, n_gz),
        out_shape=(
            shape((ext, width), f32),
            shape((ext, width), f32),
            shape((FIRST_ROWS * triple, first_lanes), bf16),
            shape((DOWN_ROWS * channels, triple * (2 * DOWN_ROWS + 1)), bf16),
            shape((DEEP_ROWS * channels, triple * (DEEP_ROWS + 2)), bf16),
            shape((LAST_ROWS * channels, triple * (LAST_ROWS + 2)), bf16),
        ),
        in_specs=[smem] * 5 + [vmem] * 3,
        out_specs=(vmem,) * 6,
        scratch_shapes=[
            pltpu.VMEM((2 * REACH + 2, tile, width), bf16),
            pltpu.VMEM((ext, width), f32),
            pltpu.VMEM((ext, width), f32),
            pltpu.VMEM((ext, width), f32),
            pltpu.SemaphoreType.DMA((2 * REACH + 2,)),
            pltpu.SemaphoreType.DMA((2 * REACH + 2,)),
            pltpu.SemaphoreType.DMA((2,)),
            pltpu.SemaphoreType.DMA((2,)),
            pltpu.SemaphoreType.DMA((pieces + 2,)),
            pltpu.SemaphoreType.DMA((pieces + 2,)),
        ],
        compiler_params=pltpu.CompilerParams(
            collective_id=0, has_side_effects=True, vmem_limit_bytes=40 * 1024 * 1024
        ),
    )(block_offset, row_base, col_base, fractions, blend, section, base_first, base)

    hidden_rows = ceil_div(tile + 9, FIRST_ROWS) * FIRST_ROWS
    down_rows = ceil_div(out_rows + 4, DOWN_ROWS) * DOWN_ROWS
    deep_rows = ceil_div(out_rows + 2, DEEP_ROWS) * DEEP_ROWS
    features = pl.pallas_call(
        functools.partial(encoder_kernel, n_rows),
        out_shape=shape((channels, out_rows, half), bf16),
        in_specs=[vmem] * 7,
        out_specs=vmem,
        scratch_shapes=[
            pltpu.VMEM((half // LANES, ext * SLOTS, LANES), f32),
            pltpu.VMEM((hidden_rows, triple, half), bf16),
            pltpu.VMEM((down_rows, triple, half), bf16),
            pltpu.VMEM((deep_rows, triple, half), bf16),
        ],
        compiler_params=pltpu.CompilerParams(vmem_limit_bytes=48 * 1024 * 1024),
    )(warped, prior, first, down, deep, last, biases)
    return features[None, None]


def solution(mesh):
    return jax.shard_map(
        functools.partial(per_device, mesh.shape["rows"], mesh.shape["gz"]),
        mesh=mesh,
        in_specs=(
            P(None, "gz", "rows", None),
            P(None, "gz", "rows", None),
            P(None, "gz", "rows", None),
            P(None, "gz", "rows", None),
            P(None, None, "gz", "rows", None),
            P(None, "gz"),
            P(),
            P(),
            P(),
            P(),
            P(),
            P(),
        ),
        out_specs=P(None, "gz", None, "rows", None),
        check_vma=False,
    )
```

```python
import functools

import jax
import jax.numpy as jnp
from jax import lax
from jax.experimental import pallas as pl
from jax.experimental.pallas import tpu as pltpu
from jax.sharding import PartitionSpec as P

REACH = 3
HALO = 8
FIRST_ROWS = 14
DOWN_ROWS = 4
DEEP_ROWS = 6
LAST_ROWS = 8
SLOTS = 16
LANES = 128
MESH = pl.DeviceIdType.MESH


def ceil_div(a, b):
    return -(-a // b)


def exchange_kernel(
    n_rows,
    n_gz,
    offset_ref,
    row_ref,
    col_ref,
    fraction_ref,
    blend_ref,
    section_ref,
    bias_in,
    conv_first_in,
    conv_down_in,
    conv_deep_in,
    warped_ref,
    prior_ref,
    first_ref,
    down_ref,
    deep_ref,
    last_ref,
    bias_ref,
    source,
    warped,
    prior,
    state,
    sec_send,
    sec_recv,
    halo_send,
    halo_recv,
    chain_send,
    chain_recv,
    bias_raw,
    conv_first_raw,
    conv_down_raw,
    conv_deep_raw,
    load_sem,
):
    me = lax.axis_index("rows")
    z = lax.axis_index("gz")
    tile, width = section_ref.shape
    half = width // 2
    load_section = pltpu.make_async_copy(section_ref, source.at[REACH], load_sem.at[0])
    load_section.start()
    loads = [
        pltpu.make_async_copy(src, dst, load_sem.at[1 + index])
        for index, (src, dst) in enumerate(
            (
                (bias_in, bias_raw),
                (conv_first_in, conv_first_raw),
                (conv_down_in, conv_down_raw),
                (conv_deep_in, conv_deep_raw),
            )
        )
    ]
    for load in loads:
        load.start()
    odd = lax.rem(me, 2)
    even = 1 - odd
    sibling = me + even - odd

    barrier = pltpu.get_barrier_semaphore()
    greeted = jnp.int32(0)
    for d in (-4, -3, -2, -1, 1, 2, 3, 4):
        ok = jnp.logical_and(me + d >= 0, me + d < n_rows)

        @pl.when(ok)
        def _(d=d):
            pl.semaphore_signal(barrier, inc=1, device_id=(z, me + d), device_id_type=MESH)

        greeted = greeted + jnp.where(ok, 1, 0)
    for d in (-1, 1):
        ok = jnp.logical_and(z + d >= 0, z + d < n_gz)

        @pl.when(ok)
        def _(d=d):
            pl.semaphore_signal(barrier, inc=1, device_id=(z + d, me), device_id_type=MESH)

        greeted = greeted + jnp.where(ok, 1, 0)

    load_section.wait()
    pl.semaphore_wait(barrier, greeted)

    def send(src_slot, dst_slot, target):
        return pltpu.make_async_remote_copy(
            src_ref=source.at[src_slot],
            dst_ref=source.at[dst_slot],
            send_sem=sec_send.at[dst_slot],
            recv_sem=sec_recv.at[dst_slot],
            device_id=(z, target),
            device_id_type=MESH,
        )

    def inside(k):
        return jnp.logical_and(k >= 0, k < n_rows)

    direct = []
    for slot in (5, 1, 7):
        target = me - (slot - REACH)
        direct.append((inside(target), send(REACH, slot, target)))
    direct.append((jnp.logical_and(odd == 1, inside(me + 3)), send(REACH, 0, me + 3)))
    relay_even = {s: (jnp.logical_and(even == 1, inside(me + s - REACH)), send(s, s - 1, sibling)) for s in (3, 5, 1, 7)}
    relay_odd = {s: (jnp.logical_and(odd == 1, inside(me + s - REACH)), send(s, s + 1, sibling)) for s in (3, 5, 1)}
    sends = direct + list(relay_even.values()) + list(relay_odd.values())

    for ok, copy in direct + [relay_even[3], relay_odd[3]]:

        @pl.when(ok)
        def _(copy=copy):
            copy.start()

    for slot in range(2 * REACH + 2):
        if slot != REACH:

            @pl.when(jnp.logical_not(inside(me + slot - REACH)))
            def _(slot=slot):
                source[slot] = jnp.zeros((tile, width), source.dtype)

    def arrive(slot):
        @pl.when(inside(me + slot - REACH))
        def _():
            send(slot, slot, sibling).wait_recv()

    def weights():
        for load in loads:
            load.wait()
        channels = conv_down_raw.shape[1]
        triple = 3 * channels
        eye = lax.broadcasted_iota(jnp.int32, (channels, channels), 0) == lax.broadcasted_iota(
            jnp.int32, (channels, channels), 1
        )

        def column(index):
            return jnp.sum(jnp.where(eye, bias_raw[index : index + 1, :], 0.0), axis=1, keepdims=True)

        for layer in range(3):
            bias_ref[layer] = jnp.broadcast_to(column(3 + layer), (channels, half))

        lanes = first_ref.shape[1]
        lane = lax.broadcasted_iota(jnp.int32, (channels, lanes), 1)
        planes = []
        for plane, slots in enumerate(((0, 1, 2), (1, 3, 4), (3, 4, 5))):
            base = jnp.zeros((channels, lanes), jnp.float32)
            for dr in range(3):
                for dx, slot in enumerate(slots):
                    tap = conv_first_raw[3 * dr + dx].astype(jnp.float32)
                    for ch in range(2):
                        base = jnp.where(lane == SLOTS * dr + 2 * slot + ch, tap[:, ch : ch + 1], base)
                base = jnp.where(lane == SLOTS * dr + (13 if plane == 0 else 12), column(dr), base)
            planes.append(base)
        base = jnp.concatenate(planes, axis=0)
        for r in range(FIRST_ROWS):
            moved = base if r == 0 else pltpu.roll(base, SLOTS * r, 1)
            first_ref[r * triple : (r + 1) * triple, :] = moved.astype(jnp.bfloat16)

        lanes = ceil_div(triple * (LAST_ROWS + 2), LANES) * LANES

        def base_of(taps):
            parts = [taps(t).astype(jnp.float32) for t in range(9)]
            rest = jnp.zeros((channels, lanes - 9 * channels), jnp.float32)
            return jnp.concatenate(parts + [rest], axis=1)

        down_base = base_of(lambda t: conv_down_raw[t])
        deep_base = base_of(lambda t: conv_deep_raw[0, t])
        last_base = base_of(lambda t: conv_deep_raw[1, t])
        for ref, base, count, step in ((down_ref, down_base, DOWN_ROWS, 2), (deep_ref, deep_base, DEEP_ROWS, 1)):
            for r in range(count):
                moved = base if r == 0 else pltpu.roll(base, triple * step * r, 1)
                ref[r * channels : (r + 1) * channels, :] = moved[:, : ref.shape[1]].astype(jnp.bfloat16)
        pieces = [last_base if r == 0 else pltpu.roll(last_base, triple * r, 1) for r in range(LAST_ROWS)]
        last = jnp.stack(pieces, axis=1).reshape(channels * LAST_ROWS, lanes)
        last_ref[...] = last[:, : last_ref.shape[1]].astype(jnp.bfloat16)

    weights()

    for slot in (5, 1, 7):
        arrive(slot)

        @pl.when(relay_even[slot][0])
        def _(slot=slot):
            relay_even[slot][1].start()

        if slot in relay_odd:

            @pl.when(relay_odd[slot][0])
            def _(slot=slot):
                relay_odd[slot][1].start()

    for slot in (4, 2, 0, 6):
        arrive(slot)

    col_tiles = width // tile
    for m in range(col_tiles // 2):
        row_parts = []
        moved_parts = []
        for side in range(2):
            j = 2 * m + side
            a = row_ref[0, 0, 0, j]
            b = col_ref[0, 0, 0, j]
            p = fraction_ref[0, 0, 0, 0, j].astype(jnp.float32) / 256.0
            q = fraction_ref[1, 0, 0, 0, j].astype(jnp.float32) / 256.0
            low = max(j - 1, 0) * tile
            high = min(j + 2, col_tiles) * tile
            window = source[pl.ds(offset_ref[0, 0, 0, j] + REACH, 2), :, low:high].reshape(2 * tile, high - low)
            src = lax.broadcasted_iota(jnp.int32, (high - low, 2 * tile), 0) + low
            lane = lax.broadcasted_iota(jnp.int32, (high - low, 2 * tile), 1)
            is_odd = lane >= tile
            place = jnp.where(is_odd, lane - tile, lane) - side * (tile // 2)
            here = jnp.logical_and(place >= 0, place < tile // 2)
            want = jnp.where(here, 2 * place + jnp.where(is_odd, 1, 0) + (j * tile + b), -(1 << 20))
            delta = src - want
            col_matrix = jnp.where(delta == 0, 1.0 - q, 0.0) + jnp.where(delta == 1, q, 0.0)
            moved = jnp.dot(window, col_matrix.astype(jnp.bfloat16), preferred_element_type=jnp.float32)
            moved_parts.append(moved.astype(jnp.bfloat16))
            delta = (
                lax.broadcasted_iota(jnp.int32, (tile, 2 * tile), 1)
                - lax.broadcasted_iota(jnp.int32, (tile, 2 * tile), 0)
                - a
            )
            row_matrix = jnp.where(delta == 0, 1.0 - p, 0.0) + jnp.where(delta == 1, p, 0.0)
            row_parts.append(row_matrix.astype(jnp.bfloat16))
        block = jnp.dot(
            jnp.concatenate(row_parts, axis=1),
            jnp.concatenate(moved_parts, axis=0),
            preferred_element_type=jnp.float32,
        )
        warped[HALO : HALO + tile, m * tile : (m + 1) * tile] = block[:, :tile]
        warped[HALO : HALO + tile, half + m * tile : half + (m + 1) * tile] = block[:, tile:]

    top = pl.ds(0, HALO)
    bottom = pl.ds(HALO + tile, HALO)

    def edge(index, src, dst, target):
        return pltpu.make_async_remote_copy(
            src_ref=warped.at[src],
            dst_ref=warped.at[dst],
            send_sem=halo_send.at[index],
            recv_sem=halo_recv.at[index],
            device_id=(z, target),
            device_id_type=MESH,
        )

    up = edge(0, pl.ds(HALO, HALO), bottom, me - 1)
    down = edge(1, pl.ds(tile, HALO), top, me + 1)
    has_up = me > 0
    has_down = me < n_rows - 1

    @pl.when(has_up)
    def _():
        up.start()

    @pl.when(has_down)
    def _():
        down.start()

    @pl.when(jnp.logical_not(has_up))
    def _():
        warped[top, :] = jnp.zeros((HALO, width), jnp.float32)

    @pl.when(jnp.logical_not(has_down))
    def _():
        warped[bottom, :] = jnp.zeros((HALO, width), jnp.float32)

    keep = blend_ref[0, 0]
    pieces = chain_send.shape[0] - 2
    length = tile // pieces
    chunks = [pl.ds(HALO + c * length, length) for c in range(pieces)] + [top, bottom]
    has_before = z > 0
    has_after = z < n_gz - 1

    def pass_on(index, chunk):
        return pltpu.make_async_remote_copy(
            src_ref=state.at[chunk],
            dst_ref=prior.at[chunk],
            send_sem=chain_send.at[index],
            recv_sem=chain_recv.at[index],
            device_id=(z + 1, me),
            device_id_type=MESH,
        )

    for index, chunk in enumerate(chunks):
        if index == pieces:

            @pl.when(has_down)
            def _():
                up.wait_recv()

            @pl.when(has_up)
            def _():
                down.wait_recv()

        @pl.when(has_before)
        def _(index=index, chunk=chunk):
            pass_on(index, chunk).wait_recv()

        @pl.when(jnp.logical_not(has_before))
        def _(chunk=chunk):
            prior[chunk, :] = jnp.zeros((chunk.size, width), jnp.float32)

        @pl.when(has_after)
        def _(index=index, chunk=chunk):
            state[chunk, :] = keep * prior[chunk, :] + (1.0 - keep) * warped[chunk, :]
            pass_on(index, chunk).start()

    warped_ref[...] = warped[...]
    prior_ref[...] = prior[...]

    for ok, copy in sends:

        @pl.when(ok)
        def _(copy=copy):
            copy.wait_send()

    @pl.when(has_up)
    def _():
        up.wait_send()

    @pl.when(has_down)
    def _():
        down.wait_send()

    @pl.when(has_after)
    def _():
        for index, chunk in enumerate(chunks):
            pass_on(index, chunk).wait_send()


def encoder_kernel(
    n_rows,
    warped_ref,
    prior_ref,
    first_ref,
    down_ref,
    deep_ref,
    last_ref,
    bias_ref,
    out_ref,
    planes,
    hidden,
    down,
    deep,
):
    me = lax.axis_index("rows")
    is_top = me == 0
    is_bottom = me == n_rows - 1
    ext, width = warped_ref.shape
    tile = ext - 2 * HALO
    half = width // 2
    channels, out_rows, _ = out_ref.shape

    def put(slot, value):
        for h in range(half // LANES):
            planes[h, pl.ds(slot, ext, stride=SLOTS), :] = value[:, h * LANES : (h + 1) * LANES]

    lane = lax.broadcasted_iota(jnp.int32, (ext, half), 1)
    zero = jnp.zeros((ext, half), jnp.float32)
    one = jnp.ones((ext, half), jnp.float32)
    for ch, ref in enumerate((warped_ref, prior_ref)):
        e = ref[:, :half]
        o = ref[:, half:]
        put(ch, jnp.where(lane == 0, 0.0, pltpu.roll(e, 1, 1)))
        put(2 + ch, jnp.where(lane == 0, 0.0, pltpu.roll(o, 1, 1)))
        put(4 + ch, jnp.where(lane == 0, 0.0, e))
        put(6 + ch, e)
        put(8 + ch, o)
        put(10 + ch, jnp.where(lane == half - 1, 0.0, pltpu.roll(e, half - 1, 1)))
        put(12 + ch, one if ch == 0 else jnp.where(lane == 0, 0.0, one))
        put(14 + ch, zero)

    def first_group(g):
        start = (2 + FIRST_ROWS * g) * SLOTS
        parts = [planes[h, pl.ds(start, SLOTS * (FIRST_ROWS + 2)), :] for h in range(half // LANES)]
        window = jnp.concatenate(parts, axis=1).astype(jnp.bfloat16)
        value = jnp.dot(first_ref[...], window, preferred_element_type=jnp.float32)
        value = jnp.maximum(value, 0.0).astype(jnp.bfloat16)
        hidden[pl.ds(g * FIRST_ROWS, FIRST_ROWS)] = value.reshape(FIRST_ROWS, 3 * channels, half)

    for g in range(hidden.shape[0] // FIRST_ROWS):
        first_group(g)

    def clear(ref, above, inner):
        @pl.when(is_top)
        def _():
            ref[0:above] = jnp.zeros((above,) + ref.shape[1:], ref.dtype)

        @pl.when(is_bottom)
        def _():
            below = ref.shape[0] - above - inner
            ref[above + inner :] = jnp.zeros((below,) + ref.shape[1:], ref.dtype)

    clear(hidden, 5, tile)

    def spread(ref, start, count, value):
        value = jnp.maximum(value, 0.0)
        lane = lax.broadcasted_iota(jnp.int32, value.shape, 1)
        left = jnp.where(lane == 0, 0.0, pltpu.roll(value, 1, 1))
        right = jnp.where(lane == half - 1, 0.0, pltpu.roll(value, half - 1, 1))
        for index, piece in enumerate((left, value, right)):
            ref[pl.ds(start, count), index * channels : (index + 1) * channels, :] = piece.astype(
                jnp.bfloat16
            ).reshape(count, channels, half)

    def biased(value, layer, count):
        return (value.reshape(count, channels, half) + bias_ref[layer][None]).reshape(count * channels, half)

    def down_group(g):
        window = hidden[pl.ds(2 * DOWN_ROWS * g, 2 * DOWN_ROWS + 1)].reshape(-1, half)
        value = jnp.dot(down_ref[...], window, preferred_element_type=jnp.float32)
        spread(down, g * DOWN_ROWS, DOWN_ROWS, biased(value, 0, DOWN_ROWS))

    for g in range(down.shape[0] // DOWN_ROWS):
        down_group(g)
    clear(down, 2, out_rows)

    def deep_group(g):
        window = down[pl.ds(DEEP_ROWS * g, DEEP_ROWS + 2)].reshape(-1, half)
        value = jnp.dot(deep_ref[...], window, preferred_element_type=jnp.float32)
        spread(deep, g * DEEP_ROWS, DEEP_ROWS, biased(value, 1, DEEP_ROWS))

    for g in range(deep.shape[0] // DEEP_ROWS):
        deep_group(g)
    clear(deep, 1, out_rows)

    for g in range(out_rows // (2 * LAST_ROWS)):
        parts = []
        for k in range(2):
            start = (2 * g + k) * LAST_ROWS
            window = deep[start : start + LAST_ROWS + 2].reshape(-1, half)
            value = jnp.dot(last_ref[...], window, preferred_element_type=jnp.float32)
            parts.append(value.reshape(channels, LAST_ROWS, half) + bias_ref[2][:, None, :])
        out_ref[:, 2 * g * LAST_ROWS : 2 * (g + 1) * LAST_ROWS, :] = jnp.concatenate(parts, axis=1).astype(
            jnp.bfloat16
        )


def per_device(
    n_rows,
    n_gz,
    sections,
    block_offset,
    row_base,
    col_base,
    fractions,
    blend,
    conv_first,
    bias_first,
    conv_down,
    bias_down,
    conv_deep,
    bias_deep,
):
    section = sections[0, 0]
    tile, width = section.shape
    half = width // 2
    out_rows = tile // 2
    channels = conv_first.shape[1]
    triple = 3 * channels
    ext = tile + 2 * HALO
    high = lax.reduce_precision(bias_first, 8, 7)
    middle = lax.reduce_precision(bias_first - high, 8, 7)
    low = bias_first - high - middle
    biases = jnp.stack([high, middle, low, bias_down, bias_deep[0], bias_deep[1]])
    first_lanes = (FIRST_ROWS + 2) * SLOTS

    vmem = pl.BlockSpec(memory_space=pltpu.VMEM)
    smem = pl.BlockSpec(memory_space=pltpu.SMEM)
    hbm = pl.BlockSpec(memory_space=pl.ANY)
    pieces = 8
    f32 = jnp.float32
    bf16 = jnp.bfloat16
    shape = jax.ShapeDtypeStruct
    warped, prior, first, down, deep, last, bias = pl.pallas_call(
        functools.partial(exchange_kernel, n_rows, n_gz),
        out_shape=(
            shape((ext, width), f32),
            shape((ext, width), f32),
            shape((FIRST_ROWS * triple, first_lanes), bf16),
            shape((DOWN_ROWS * channels, triple * (2 * DOWN_ROWS + 1)), bf16),
            shape((DEEP_ROWS * channels, triple * (DEEP_ROWS + 2)), bf16),
            shape((LAST_ROWS * channels, triple * (LAST_ROWS + 2)), bf16),
            shape((3, channels, half), f32),
        ),
        in_specs=[smem] * 5 + [hbm] * 5,
        out_specs=(vmem,) * 7,
        scratch_shapes=[
            pltpu.VMEM((2 * REACH + 2, tile, width), bf16),
            pltpu.VMEM((ext, width), f32),
            pltpu.VMEM((ext, width), f32),
            pltpu.VMEM((ext, width), f32),
            pltpu.SemaphoreType.DMA((2 * REACH + 2,)),
            pltpu.SemaphoreType.DMA((2 * REACH + 2,)),
            pltpu.SemaphoreType.DMA((2,)),
            pltpu.SemaphoreType.DMA((2,)),
            pltpu.SemaphoreType.DMA((pieces + 2,)),
            pltpu.SemaphoreType.DMA((pieces + 2,)),
            pltpu.VMEM(biases.shape, f32),
            pltpu.VMEM(conv_first.shape, bf16),
            pltpu.VMEM(conv_down.shape, bf16),
            pltpu.VMEM(conv_deep.shape, bf16),
            pltpu.SemaphoreType.DMA((5,)),
        ],
        compiler_params=pltpu.CompilerParams(
            collective_id=0, has_side_effects=True, vmem_limit_bytes=40 * 1024 * 1024
        ),
    )(block_offset, row_base, col_base, fractions, blend, section, biases, conv_first, conv_down, conv_deep)

    hidden_rows = ceil_div(tile + 9, FIRST_ROWS) * FIRST_ROWS
    down_rows = ceil_div(out_rows + 4, DOWN_ROWS) * DOWN_ROWS
    deep_rows = ceil_div(out_rows + 2, DEEP_ROWS) * DEEP_ROWS
    features = pl.pallas_call(
        functools.partial(encoder_kernel, n_rows),
        out_shape=shape((channels, out_rows, half), bf16),
        in_specs=[vmem] * 7,
        out_specs=vmem,
        scratch_shapes=[
            pltpu.VMEM((half // LANES, ext * SLOTS, LANES), f32),
            pltpu.VMEM((hidden_rows, triple, half), bf16),
            pltpu.VMEM((down_rows, triple, half), bf16),
            pltpu.VMEM((deep_rows, triple, half), bf16),
        ],
        compiler_params=pltpu.CompilerParams(vmem_limit_bytes=48 * 1024 * 1024),
    )(warped, prior, first, down, deep, last, bias)
    return features[None, None]


def solution(mesh):
    return jax.shard_map(
        functools.partial(per_device, mesh.shape["rows"], mesh.shape["gz"]),
        mesh=mesh,
        in_specs=(
            P(None, "gz", "rows", None),
            P(None, "gz", "rows", None),
            P(None, "gz", "rows", None),
            P(None, "gz", "rows", None),
            P(None, None, "gz", "rows", None),
            P(None, "gz"),
            P(),
            P(),
            P(),
            P(),
            P(),
            P(),
        ),
        out_specs=P(None, "gz", None, "rows", None),
        check_vma=False,
    )
```
